128 devices in a mesh: sample: 32 (over x, y, core), axial: 4 (over z).
Axes of the slice: x: 4, y: 4, z: 4, core: 2. Of those that a mesh axis runs over, the one named last changes fastest.
Arguments:
- pair: bfloat16 [32, 256, 256, 128], P('sample', 'axial'), may hold values from -6 to 6
- lengths: int32 [32], replicated, may hold values from 85 to 256, as said below
- block_group: int32 [32, 32], replicated, may hold values from 0 to 31, as said below
- w_proj: bfloat16 [128, 512], replicated
- w_bias: bfloat16 [128, 4], replicated
- w_out: bfloat16 [128, 128], replicated, may hold values from -1.5 to 1.5
- w_up: bfloat16 [128, 512], replicated, may hold values from -0.5 to 0.5
- w_down: bfloat16 [512, 128], replicated, may hold values from -0.25 to 0.25
Outputs:
- pair_out: bfloat16 [32, 4, 32, 2, 256, 128], P('sample', 'axial')
The draws below stay inside these ranges and needn't reach their ends.
Inputs may be any that keep to these rules, and one draw needn't show every extreme that they name: lengths run from 85 to 256; some crop has exactly 256 residues. Each row and each column of block_group names every group once.
All inputs are finite; a program needn't handle non-finite values.
Results may differ from the reference program's by a relative error of at most 0.0085.
Values may be sent and summed in bfloat16 or wider, within the bound.
No kernel may reach another device: no remote copies, remote signals or barrier semaphores. Data moves between devices by JAX's collectives and lax.ppermute only.
A program may use at most 128 MiB of HBM per device.

```python
import jax
import jax.numpy as jnp
from jax import lax

C = 128
H = 4
DH = 32
FF = 512
L = 256
CROPS = 32
BLK_ROWS = 2
N_SAMPLE = 32
N_AXIAL = 4


def draw_lengths(key, part):
    key = jax.random.fold_in(key, 1)
    first, second = jax.random.split(key)
    drawn = jax.random.randint(first, (CROPS,), L // 3, L + 1)
    chosen = jax.random.randint(second, (), 0, CROPS)
    return drawn.at[chosen].set(L).astype(jnp.int32)


def draw_block_group(key, part):
    key = jax.random.fold_in(key, 2)
    first, second = jax.random.split(key)
    shift_b = jax.random.permutation(first, N_SAMPLE)
    shift_s = jax.random.permutation(second, CROPS)
    return ((shift_b[None, :] + shift_s[:, None]) % N_SAMPLE).astype(jnp.int32)


def draw_w_bias(key, part):
    key = jax.random.fold_in(key, 3)
    base = jax.random.normal(key, (C, H), jnp.float32)
    return (base * C ** (-0.5)).astype(jnp.bfloat16)


def draw_w_proj(key, part):
    key = jax.random.fold_in(key, 4)
    first = jax.random.fold_in(key, 0)
    inner = H * DH
    base = jax.random.normal(first, (C, 4 * inner), jnp.float32) * C ** (-0.5)
    return base.astype(jnp.bfloat16)


def level_of(key, shape, shards, low, largest):
    loudness = 1.0
    for position, shards_of in shards:
        heights = jax.random.uniform(jax.random.fold_in(jax.random.fold_in(key, 6), position), (shards_of,), jnp.float32, low / len(shards), largest / len(shards))
        loudness = loudness * jnp.repeat(jnp.exp(heights), shape[position] // shards_of).reshape((-1,) + (1,) * (len(shape) - 1 - position))
    return loudness


def bell_draw(stream_key, dims, width, reach, cuts=(), held_as=jnp.bfloat16):
    entries = width * jax.random.normal(stream_key, dims, jnp.float32)
    if cuts:
        entries = entries * level_of(stream_key, dims, cuts, -0.22, 0.18)
    return jnp.clip(entries, -reach, reach).astype(held_as)


def setup_inputs(seed: int = 0) -> dict:
    splits = jax.random.split(jax.random.key(seed), 9)
    return {
        "pair": bell_draw(splits[0], (CROPS, L, L, C), 1.0, 6.0, ((0, 32), (1, 4))),
        "lengths": draw_lengths(jax.random.fold_in(splits[8], 71), 0),
        "block_group": draw_block_group(jax.random.fold_in(splits[8], 71), 0),
        "w_proj": draw_w_proj(jax.random.fold_in(splits[8], 71), 0),
        "w_bias": draw_w_bias(jax.random.fold_in(splits[8], 71), 0),
        "w_out": bell_draw(splits[5], (H * DH, C), (H * DH // 8) ** -0.5, 1.5),
        "w_up": bell_draw(splits[6], (C, FF), C ** -0.5, 0.5),
        "w_down": bell_draw(splits[7], (FF, C), FF ** -0.5, 0.25),
    }


def layer_norm(values_in):
    values_in = values_in.astype(jnp.float32)
    centre = values_in - lax.optimization_barrier(jnp.mean(values_in, -1, keepdims=True))
    spread = lax.optimization_barrier(jnp.mean(centre * centre, -1, keepdims=True))
    return centre * lax.rsqrt(spread + 1e-05)

def update_rows(block, normed, bias, row_ids, length, w_proj, w_out, w_up, w_down):
    groups, rows, width_l, chans = block.shape
    heads = bias.shape[1]
    inner = w_proj.shape[1] // 4
    size_h = inner // heads
    f32 = jnp.float32
    bf16 = jnp.bfloat16
    projected = jnp.einsum('grlc,cf->grlf', normed.astype(f32), w_proj.astype(f32))
    shape_h = (groups, rows, width_l, heads, size_h)
    query = (projected[..., :inner] * size_h ** (-0.5)).astype(bf16).reshape(shape_h)
    keys = projected[..., inner:2 * inner].astype(bf16).reshape(shape_h)
    values = projected[..., 2 * inner:3 * inner].astype(bf16).reshape(shape_h)
    gate = jax.nn.sigmoid(projected[..., 3 * inner:])
    scores = jnp.einsum('grjhd,grkhd->grhjk', query.astype(f32), keys.astype(f32)) + bias[:, None].astype(f32)
    columns = jnp.arange(width_l, dtype=jnp.int32)
    key_live = columns[None, :] < length[:, None]
    scores = jnp.where(key_live[:, None, None, None, :], scores, -1000000000.0)
    weights = jax.nn.softmax(scores, axis=-1).astype(bf16)
    attended = jnp.einsum('grhjk,grkhd->grjhd', weights.astype(f32), values.astype(f32)).reshape(groups, rows, width_l, inner)
    gated = (gate * attended).astype(bf16)
    update = jnp.einsum('grlf,fc->grlc', gated.astype(f32), w_out.astype(f32))
    pair_live = (row_ids < length[:, None])[:, :, None] & key_live[:, None, :]
    middle = (block.astype(f32) + jnp.where(pair_live[..., None], update, 0.0)).astype(bf16)
    middle = lax.optimization_barrier(middle)
    normed_mid = layer_norm(middle).astype(bf16)
    hidden = jax.nn.relu(jnp.einsum('grlc,cf->grlf', normed_mid.astype(f32), w_up.astype(f32))).astype(bf16)
    down = jnp.einsum('grlf,fc->grlc', hidden.astype(f32), w_down.astype(f32))
    return (middle.astype(f32) + down).astype(bf16)

def reference(pair, lengths, block_group, w_proj, w_bias, w_out, w_up, w_down):

    def crop_update(item):
        pair_crop, length = item
        normed = layer_norm(pair_crop).astype(jnp.bfloat16)
        bias = jnp.einsum('ilc,ch->hil', normed.astype(jnp.float32), w_bias.astype(jnp.float32)).astype(jnp.bfloat16)
        blocks = pair_crop.reshape(L // 4, 1, 4, L, C)
        normeds = normed.reshape(L // 4, 1, 4, L, C)
        row_ids = jnp.arange(L, dtype=jnp.int32).reshape(L // 4, 1, 4)

        def step(part_item):
            return update_rows(part_item[0], part_item[1], bias[None], part_item[2], length[None], w_proj, w_out, w_up, w_down)
        return lax.map(step, (blocks, normeds, row_ids)).reshape(L, L, C)
    updated = lax.map(crop_update, (pair, lengths))
    shaped = updated.reshape(CROPS, N_AXIAL, N_SAMPLE, BLK_ROWS, L, C)
    groups_ids = jnp.arange(N_SAMPLE, dtype=jnp.int32)
    equal = block_group[:, None, :] == groups_ids[None, :, None]
    inverse = lax.optimization_barrier(jnp.sum(jnp.where(equal, groups_ids[None, None, :], 0), -1)).astype(jnp.int32)
    crop_ids = jnp.arange(CROPS, dtype=jnp.int32)
    picked = shaped[crop_ids[:, None], :, inverse]
    return jnp.transpose(picked, (1, 2, 0, 3, 4, 5))
```

```python
import functools

import jax
import jax.numpy as jnp
from jax import lax
from jax.experimental import pallas as pl
from jax.experimental.pallas import tpu as pltpu
from jax.sharding import PartitionSpec as P

F32 = jnp.float32
BF16 = jnp.bfloat16
LOG2E = 1.4426950408889634
DEAD = -1e9
NT = (((1,), (1,)), ((), ()))


def normalise(values_in):
    centre = values_in - jnp.mean(values_in, -1, keepdims=True)
    spread = jnp.mean(centre * centre, -1, keepdims=True)
    return centre * lax.rsqrt(spread + 1e-05)


def bias_kernel(x_ref, wb_ref, normed_ref, bias_ref, hold_ref):
    rows = x_ref.shape[0]
    heads = bias_ref.shape[0]
    for r in range(rows):
        normed = normalise(x_ref[r].astype(F32)).astype(BF16)
        normed_ref[r] = normed
        res = lax.dot_general(wb_ref[...], normed, NT, preferred_element_type=F32)
        for h in range(heads):
            hold_ref[h, r : r + 1, :] = res[h : h + 1]
    bias_ref[...] = hold_ref[...].astype(BF16)


def local_bias(local, w_bias):
    rows, width, chans = local.shape
    heads = w_bias.shape[1]
    step = 16
    wb = jnp.zeros((8, chans), BF16).at[:heads].set(w_bias.T)
    return pl.pallas_call(
        bias_kernel,
        name="bias",
        grid=(rows // step,),
        in_specs=[
            pl.BlockSpec((step, width, chans), lambda i: (i, 0, 0)),
            pl.BlockSpec((8, chans), lambda i: (0, 0)),
        ],
        out_specs=[
            pl.BlockSpec((step, width, chans), lambda i: (i, 0, 0)),
            pl.BlockSpec((heads, step, width), lambda i: (0, i, 0)),
        ],
        out_shape=[
            jax.ShapeDtypeStruct((rows, width, chans), BF16),
            jax.ShapeDtypeStruct((heads, rows, width), BF16),
        ],
        scratch_shapes=[pltpu.VMEM((heads, step, width), F32)],
        compiler_params=pltpu.CompilerParams(vmem_limit_bytes=48 * 1024 * 1024),
    )(local, wb)


def update_kernel(
    order_ref,
    info_ref,
    x_ref,
    n_ref,
    bias_ref,
    wp_ref,
    wo_ref,
    wu_ref,
    wd_ref,
    out_ref,
    bias_s,
    mid_s,
):
    step = pl.program_id(0)
    _, rows, width, chans = x_ref.shape
    heads = bias_ref.shape[0]
    inner = wp_ref.shape[1] // 4
    size_h = inner // heads
    length = info_ref[0]
    first = info_ref[1] + order_ref[step] * rows

    @pl.when(step == 0)
    def _():
        live = lax.broadcasted_iota(jnp.int32, (width, width), 1) < length
        for h in range(heads):
            bias_s[h] = jnp.where(live, bias_ref[h].astype(F32) * LOG2E, DEAD)

    lane = lax.broadcasted_iota(jnp.int32, (width, inner), 1)
    masks = [(lane >= h * size_h) & (lane < (h + 1) * size_h) for h in range(heads)]

    def attend(safe):
        bad = None
        for r in range(rows):
            normed = n_ref[0, r]
            proj = jnp.dot(normed, wp_ref[...], preferred_element_type=F32)
            query = (proj[:, :inner] * (size_h ** (-0.5) * LOG2E)).astype(BF16)
            keys = proj[:, inner : 2 * inner].astype(BF16)
            values = proj[:, 2 * inner : 3 * inner].astype(BF16)
            gate = jax.nn.sigmoid(proj[:, 3 * inner :])
            zero = jnp.zeros((), BF16)
            one = jnp.ones((), BF16)
            both = jnp.zeros((width, 2 * inner), F32)
            for h in range(heads):
                score = lax.dot_general(
                    jnp.where(masks[h], query, zero), keys, NT, preferred_element_type=F32
                )
                score = score + bias_s[h]
                if safe:
                    score = score - jnp.max(score, -1, keepdims=True)
                weight = jnp.exp2(score).astype(BF16)
                side = jnp.concatenate(
                    [jnp.where(masks[h], values, zero), jnp.where(masks[h], one, zero)], 1
                )
                both = both + jnp.dot(weight, side, preferred_element_type=F32)
            total = both[:, inner:]
            if not safe:
                low, high = jnp.min(total), jnp.max(total)
                good = (low > 1e-20) & (high < 1e30)
                bad = jnp.logical_not(good) if bad is None else bad | jnp.logical_not(good)
            gated = (gate * (both[:, :inner] / total)).astype(BF16)
            update = jnp.dot(gated, wo_ref[...], preferred_element_type=F32)
            place = lax.broadcasted_iota(jnp.int32, (width, chans), 0)
            live = (place < length) & (first + r < length)
            middle = x_ref[0, r].astype(F32) + jnp.where(live, update, 0.0)
            mid_s[r * width : (r + 1) * width] = middle.astype(BF16)
        return bad

    @pl.when(first < length)
    def _():
        bad = attend(False)

        @pl.when(bad)
        def _():
            attend(True)

    @pl.when(first >= length)
    def _():
        mid_s[...] = x_ref[0].reshape(rows * width, chans)

    middle = mid_s[...].astype(F32)
    normed_mid = normalise(middle).astype(BF16)
    hidden = jax.nn.relu(jnp.dot(normed_mid, wu_ref[...], preferred_element_type=F32)).astype(BF16)
    down = jnp.dot(hidden, wd_ref[...], preferred_element_type=F32)
    out_ref[...] = (middle + down).astype(BF16).reshape(out_ref.shape)


def update_blocks(order, info, blocks, normeds, bias, w_proj, w_out, w_up, w_down):
    count = order.shape[0]
    _, rows, width, chans = blocks.shape
    heads = bias.shape[0]
    whole = lambda *shape: pl.BlockSpec(shape, lambda i, o, n: (0,) * len(shape))
    picked = pl.BlockSpec((1, rows, width, chans), lambda i, o, n: (o[i], 0, 0, 0))
    return pl.pallas_call(
        update_kernel,
        name="update",
        grid_spec=pltpu.PrefetchScalarGridSpec(
            num_scalar_prefetch=2,
            grid=(count,),
            in_specs=[
                picked,
                picked,
                whole(heads, width, width),
                whole(*w_proj.shape),
                whole(*w_out.shape),
                whole(*w_up.shape),
                whole(*w_down.shape),
            ],
            out_specs=pl.BlockSpec((1, rows, width, chans), lambda i, o, n: (i, 0, 0, 0)),
            scratch_shapes=[
                pltpu.VMEM((heads, width, width), F32),
                pltpu.VMEM((rows * width, chans), BF16),
            ],
        ),
        out_shape=jax.ShapeDtypeStruct((count, rows, width, chans), BF16),
        compiler_params=pltpu.CompilerParams(vmem_limit_bytes=48 * 1024 * 1024),
    )(order, info, blocks, normeds, bias, w_proj, w_out, w_up, w_down)


def shards(pair, lengths, block_group, w_proj, w_bias, w_out, w_up, w_down):
    group_idx = lax.axis_index("sample")
    axial_idx = lax.axis_index("axial")
    groups_n = lax.axis_size("sample")
    _, ax_rows, width, chans = pair.shape
    blk_rows = ax_rows // groups_n
    local = pair[0]
    group_ids = jnp.arange(groups_n, dtype=jnp.int32)
    own_row = jnp.take(block_group, group_idx, axis=0)
    order = jnp.sum(jnp.where(own_row[None, :] == group_ids[:, None], group_ids[None, :], 0), 1)
    length = jnp.take(lengths, group_idx)
    info = jnp.stack([length, axial_idx * ax_rows]).astype(jnp.int32)
    normed, bias = local_bias(local, w_bias)
    crop_bias = lax.all_gather(bias, "axial", axis=1, tiled=True)
    shape = (groups_n, blk_rows, width, chans)
    updated = update_blocks(
        order, info, local.reshape(shape), normed.reshape(shape), crop_bias, w_proj, w_out, w_up, w_down
    )
    arrived = lax.all_to_all(updated, "sample", split_axis=0, concat_axis=0, tiled=True)
    return arrived.reshape(1, 1, groups_n, blk_rows, width, chans)


def solution(mesh):
    return jax.shard_map(
        shards,
        mesh=mesh,
        in_specs=(P("sample", "axial", None, None), P(), P(), P(), P(), P(), P(), P()),
        out_specs=P("sample", "axial", None, None, None, None),
        check_vma=False,
    )
```

```python
import functools

import jax
import jax.numpy as jnp
from jax import lax
from jax.experimental import pallas as pl
from jax.experimental.pallas import tpu as pltpu
from jax.sharding import PartitionSpec as P

F32 = jnp.float32
BF16 = jnp.bfloat16
LOG2E = 1.4426950408889634
DEAD = -1e9
NT = (((1,), (1,)), ((), ()))


def normalise(values_in):
    centre = values_in - jnp.mean(values_in, -1, keepdims=True)
    spread = jnp.mean(centre * centre, -1, keepdims=True)
    return centre * lax.rsqrt(spread + 1e-05)


def bias_kernel(x_hbm, wb_ref, x_ref, normed_ref, bias_ref, hold_ref, sems):
    rows = x_ref.shape[0]
    heads = bias_ref.shape[0]
    parts = sems.shape[0]
    span = rows // parts
    copies = []
    for p in range(parts):
        part = pl.ds(p * span, span)
        copies.append(pltpu.make_async_copy(x_hbm.at[part], x_ref.at[part], sems.at[p]))
        copies[-1].start()
    for p in range(parts):
        copies[p].wait()
        for r in range(p * span, (p + 1) * span):
            normed = normalise(x_ref[r].astype(F32)).astype(BF16)
            normed_ref[r] = normed
            res = lax.dot_general(wb_ref[...], normed, NT, preferred_element_type=F32)
            for h in range(heads):
                hold_ref[h, r : r + 1, :] = res[h : h + 1]
    bias_ref[...] = hold_ref[...].astype(BF16)


def local_bias(local, w_bias):
    rows, width, chans = local.shape
    heads = w_bias.shape[1]
    wb = jnp.zeros((8, chans), BF16).at[:heads].set(w_bias.T)
    vmem = pl.BlockSpec(memory_space=pltpu.VMEM)
    return pl.pallas_call(
        bias_kernel,
        name="bias",
        in_specs=[pl.BlockSpec(memory_space=pl.ANY), vmem],
        out_specs=[vmem, vmem, vmem],
        out_shape=[
            jax.ShapeDtypeStruct((rows, width, chans), BF16),
            jax.ShapeDtypeStruct((rows, width, chans), BF16),
            jax.ShapeDtypeStruct((heads, rows, width), BF16),
        ],
        scratch_shapes=[pltpu.VMEM((heads, rows, width), F32), pltpu.SemaphoreType.DMA((8,))],
        compiler_params=pltpu.CompilerParams(vmem_limit_bytes=32 * 1024 * 1024),
    )(local, wb)


def masked_bias(bias, length):
    live = jnp.arange(bias.shape[-1], dtype=jnp.int32) < length
    return jnp.where(live, bias.astype(F32) * LOG2E, DEAD)


def update_kernel(
    order_ref, info_ref, x_ref, n_ref, bias_ref, wp_ref, wo_ref, wu_ref, wd_ref, out_ref, sum_s, low_s, high_s
):
    _, rows, width, chans = x_ref.shape
    heads = bias_ref.shape[0]
    inner = wp_ref.shape[1] // 4
    size_h = inner // heads
    length = info_ref[0]
    lane = lax.broadcasted_iota(jnp.int32, (width, inner), 1)
    zero = jnp.zeros((), BF16)

    def head_mask(h):
        return (lane >= h * size_h) & (lane < (h + 1) * size_h)

    masks = [head_mask(h) for h in range(heads)]

    def project(block, r):
        proj = jnp.dot(n_ref[block, r], wp_ref[...], preferred_element_type=F32)
        query = (proj[:, :inner] * (size_h ** (-0.5) * LOG2E)).astype(BF16)
        keys = proj[:, inner : 2 * inner].astype(BF16)
        values = proj[:, 2 * inner : 3 * inner].astype(BF16)
        return query, keys, jnp.concatenate([values, jnp.ones_like(values)], 1), proj[:, 3 * inner :]

    def score_of(query, keys, mask, h):
        score = lax.dot_general(jnp.where(mask, query, zero), keys, NT, preferred_element_type=F32)
        return score + bias_ref[h]

    def weigh(score, side):
        return jnp.dot(jnp.exp2(score).astype(BF16), side, preferred_element_type=F32)

    def close(block, first, r, both, gate):
        gated = (jax.nn.sigmoid(gate) * (both[:, :inner] / both[:, inner:])).astype(BF16)
        update = jnp.dot(gated, wo_ref[...], preferred_element_type=F32)
        place = lax.broadcasted_iota(jnp.int32, (width, chans), 0)
        live = (place < length) & (first + r < length)
        middle = x_ref[block, r].astype(F32) + jnp.where(live, update, 0.0)
        return middle.astype(BF16)

    def finish(middle):
        middle = middle.astype(F32)
        normed_mid = normalise(middle).astype(BF16)
        hidden = jnp.dot(normed_mid, wu_ref[...], preferred_element_type=F32)
        hidden = jax.nn.relu(hidden).astype(BF16)
        down = jnp.dot(hidden, wd_ref[...], preferred_element_type=F32)
        return (middle + down).astype(BF16)

    def attend(i, block, first):
        ends = []
        mids = []
        for r in range(rows):
            query, keys, side, gate = project(block, r)
            both = None
            for h in range(heads):
                each = weigh(score_of(query, keys, masks[h], h), side)
                mask = jnp.concatenate([masks[h], masks[h]], 1)
                both = each if both is None else jnp.where(mask, each, both)
            mids.append(close(block, first, r, both, gate))
            ends.append(both[:, inner:])
        out_ref[i] = finish(jnp.concatenate(mids, 0)).reshape(rows, width, chans)
        low = functools.reduce(jnp.minimum, ends)
        high = functools.reduce(jnp.maximum, ends)
        low_s[...] = jnp.minimum(low_s[...], jnp.min(low.reshape(-1, 8, inner), 0))
        high_s[...] = jnp.maximum(high_s[...], jnp.max(high.reshape(-1, 8, inner), 0))

    def attend_safe(i, block, first):
        def one_row(r, carry):
            query, keys, side, gate = project(block, r)

            def one_head(h, carry):
                mask = head_mask(h)
                score = score_of(query, keys, mask, h)
                each = weigh(score - jnp.max(score, -1, keepdims=True), side)
                sum_s[...] = jnp.where(jnp.concatenate([mask, mask], 1), each, sum_s[...])
                return carry

            lax.fori_loop(0, heads, one_head, 0)
            out_ref[i, r] = finish(close(block, first, r, sum_s[...], gate))
            return carry

        lax.fori_loop(0, rows, one_row, 0)

    count = out_ref.shape[0]
    low_s[...] = jnp.ones_like(low_s)
    high_s[...] = jnp.ones_like(high_s)

    def one_block(i, carry):
        block = order_ref[i]
        first = info_ref[1] + block * rows

        @pl.when(first < length)
        def _():
            attend(i, block, first)

        @pl.when(first >= length)
        def _():
            out_ref[i] = finish(x_ref[block].reshape(rows * width, chans)).reshape(rows, width, chans)

        return carry

    lax.fori_loop(0, count, one_block, 0, unroll=1)
    good = (jnp.min(low_s[...]) > 1e-20) & (jnp.max(high_s[...]) < 1e30)

    @pl.when(jnp.logical_not(good))
    def _():
        def again(i, carry):
            block = order_ref[i]
            first = info_ref[1] + block * rows

            @pl.when(first < length)
            def _():
                attend_safe(i, block, first)

            return carry

        lax.fori_loop(0, count, again, 0)


def update_blocks(order, info, blocks, normeds, bias, w_proj, w_out, w_up, w_down):
    count = order.shape[0]
    _, rows, width, chans = blocks.shape
    vmem = pl.BlockSpec(memory_space=pltpu.VMEM)
    smem = pl.BlockSpec(memory_space=pltpu.SMEM)
    work = 2 * rows * width * chans * count * (12 * chans + 4 * width)
    return pl.pallas_call(
        update_kernel,
        name="update",
        in_specs=[smem, smem] + [vmem] * 7,
        out_specs=vmem,
        out_shape=jax.ShapeDtypeStruct((count, rows, width, chans), BF16),
        scratch_shapes=[
            pltpu.VMEM((width, w_proj.shape[1] // 2), F32),
            pltpu.VMEM((8, w_proj.shape[1] // 4), F32),
            pltpu.VMEM((8, w_proj.shape[1] // 4), F32),
        ],
        cost_estimate=pl.CostEstimate(flops=8 * work, bytes_accessed=0, transcendentals=0),
        compiler_params=pltpu.CompilerParams(vmem_limit_bytes=16 * 1024 * 1024),
    )(order, info, blocks, normeds, bias, w_proj, w_out, w_up, w_down)


def place_kernel(where_ref, *refs):
    count = where_ref.shape[0]
    parts, out_ref, sems = refs[:count], refs[count], refs[count + 1]
    copies = [
        pltpu.make_async_copy(parts[t], out_ref.at[pl.ds(where_ref[t], 1)], sems.at[t])
        for t in range(count)
    ]
    for copy in copies:
        copy.start()
    for copy in copies:
        copy.wait()


def place_parts(where, parts):
    anywhere = pl.BlockSpec(memory_space=pl.ANY)
    count = len(parts)
    return pl.pallas_call(
        place_kernel,
        name="place",
        in_specs=[pl.BlockSpec(memory_space=pltpu.SMEM)] + [anywhere] * count,
        out_specs=anywhere,
        out_shape=jax.ShapeDtypeStruct((count,) + parts[0].shape[1:], BF16),
        scratch_shapes=[pltpu.SemaphoreType.DMA((count,))],
    )(where, *parts)


def shift_order():
    pairs = [(1, 1), (3, 3), (1, 3), (3, 1), (2, 0), (0, 2), (1, 0), (3, 0), (0, 1), (0, 3)]
    pairs += [(2, 1), (2, 3), (1, 2), (3, 2), (2, 2), (0, 0)]
    return [(dx, dy, dc) for dx, dy in pairs for dc in (1, 0)]


def moved(group, shift, sign):
    dx, dy, dc = shift
    x, y, c = group // 8, (group // 2) % 4, group % 2
    return (((x + sign * dx) % 4) * 4 + (y + sign * dy) % 4) * 2 + (c + dc) % 2


def shards(pair, lengths, block_group, w_proj, w_bias, w_out, w_up, w_down):
    group_idx = lax.axis_index("sample")
    axial_idx = lax.axis_index("axial")
    groups_n = lax.axis_size("sample")
    _, ax_rows, width, chans = pair.shape
    blk_rows = ax_rows // groups_n
    local = pair[0]
    group_ids = jnp.arange(groups_n, dtype=jnp.int32)
    own_row = jnp.take(block_group, group_idx, axis=0)
    shifts = shift_order()
    steps = jnp.asarray(shifts, jnp.int32)
    targets = moved(group_idx, steps.T, 1)
    sources = moved(group_idx, steps.T, -1).astype(jnp.int32)
    order = jnp.sum(jnp.where(own_row[None, :] == targets[:, None], group_ids[None, :], 0), 1)
    length = jnp.take(lengths, group_idx)
    info = jnp.stack([length, axial_idx * ax_rows]).astype(jnp.int32)
    local, normed, bias = local_bias(local, w_bias)
    crop_bias = masked_bias(lax.all_gather(bias, "axial", axis=1, tiled=True), length)
    shape = (groups_n, blk_rows, width, chans)
    local, normed = local.reshape(shape), normed.reshape(shape)
    parts = []
    span = 4
    for start in range(0, groups_n, span):
        updated = update_blocks(
            order[start : start + span],
            info,
            local,
            normed,
            crop_bias,
            w_proj,
            w_out,
            w_up,
            w_down,
        )
        if start >= span:
            before = parts[start - span : start]
            info, updated, before = lax.optimization_barrier((info, updated, before))
            parts[start - span : start] = before
        else:
            info, updated = lax.optimization_barrier((info, updated))
        for t in range(start, start + span):
            part = updated[t - start : t - start + 1]
            if any(shifts[t]):
                pairs = [(g, moved(g, shifts[t], 1)) for g in range(groups_n)]
                part = lax.ppermute(part, "sample", pairs)
            parts.append(part)
    out = place_parts(sources, parts)
    return out.reshape(1, 1, groups_n, blk_rows, width, chans)


def solution(mesh):
    return jax.shard_map(
        shards,
        mesh=mesh,
        in_specs=(P("sample", "axial", None, None), P(), P(), P(), P(), P(), P(), P()),
        out_specs=P("sample", "axial", None, None, None, None),
        check_vma=False,
    )
```

```python
import functools

import jax
import jax.numpy as jnp
from jax import lax
from jax.experimental import pallas as pl
from jax.experimental.pallas import tpu as pltpu
from jax.sharding import PartitionSpec as P

F32 = jnp.float32
BF16 = jnp.bfloat16
LOG2E = 1.4426950408889634
DEAD = -1e9
NT = (((1,), (1,)), ((), ()))


def normalise(values_in):
    centre = values_in - jnp.mean(values_in, -1, keepdims=True)
    spread = jnp.mean(centre * centre, -1, keepdims=True)
    return centre * lax.rsqrt(spread + 1e-05)


def bias_kernel(
    keep_at_ref, send_at_ref, x_hbm, wb_ref, keep_ref, send_ref, bias_ref, x_ref, normed_ref, hold_ref, sems
):
    rows = x_ref.shape[0]
    _, count, blk_rows, _, _ = keep_ref.shape
    heads = bias_ref.shape[0]
    parts = sems.shape[0]
    span = rows // parts
    copies = []
    for p in range(parts):
        part = pl.ds(p * span, span)
        copies.append(pltpu.make_async_copy(x_hbm.at[part], x_ref.at[part], sems.at[p]))
        copies[-1].start()
    for p in range(parts):
        copies[p].wait()
        for r in range(p * span, (p + 1) * span):
            normed = normalise(x_ref[r].astype(F32)).astype(BF16)
            normed_ref[r] = normed
            res = lax.dot_general(wb_ref[...], normed, NT, preferred_element_type=F32)
            for h in range(heads):
                hold_ref[h, r : r + 1, :] = res[h : h + 1]
    bias_ref[...] = hold_ref[...].astype(BF16)

    def sort(t, carry):
        for at_ref, to_ref in ((keep_at_ref, keep_ref), (send_at_ref, send_ref)):
            part = pl.ds(at_ref[t] * blk_rows, blk_rows)
            to_ref[0, t] = x_ref[part]
            to_ref[1, t] = normed_ref[part]
        return carry

    lax.fori_loop(0, count, sort, 0)


def local_bias(keep_at, send_at, local, w_bias):
    rows, width, chans = local.shape
    heads = w_bias.shape[1]
    count = keep_at.shape[0]
    wb = jnp.zeros((8, chans), BF16).at[:heads].set(w_bias.T)
    vmem = pl.BlockSpec(memory_space=pltpu.VMEM)
    smem = pl.BlockSpec(memory_space=pltpu.SMEM)
    blocks = jax.ShapeDtypeStruct((2, count, rows // (2 * count), width, chans), BF16)
    return pl.pallas_call(
        bias_kernel,
        name="bias",
        in_specs=[smem, smem, pl.BlockSpec(memory_space=pl.ANY), vmem],
        out_specs=[vmem, vmem, vmem],
        out_shape=[blocks, blocks, jax.ShapeDtypeStruct((heads, rows, width), BF16)],
        scratch_shapes=[
            pltpu.VMEM((rows, width, chans), BF16),
            pltpu.VMEM((rows, width, chans), BF16),
            pltpu.VMEM((heads, rows, width), F32),
            pltpu.SemaphoreType.DMA((8,)),
        ],
        compiler_params=pltpu.CompilerParams(vmem_limit_bytes=32 * 1024 * 1024),
    )(keep_at, send_at, local, wb)


def join_kernel(where_ref, *refs):
    parts, out_ref = refs[:-1], refs[-1]
    rows = parts[0].shape[1]
    for t, part in enumerate(parts):
        out_ref[:, pl.ds(pl.multiple_of(where_ref[t] * rows, rows), rows), :] = part[...]


def join_bias(where, parts):
    heads, rows, width = parts[0].shape
    vmem = pl.BlockSpec(memory_space=pltpu.VMEM)
    return pl.pallas_call(
        join_kernel,
        name="join",
        in_specs=[pl.BlockSpec(memory_space=pltpu.SMEM)] + [vmem] * len(parts),
        out_specs=vmem,
        out_shape=jax.ShapeDtypeStruct((heads, rows * len(parts), width), BF16),
    )(where, *parts)


def masked_bias(bias, length):
    live = jnp.arange(bias.shape[-1], dtype=jnp.int32) < length
    return jnp.where(live, bias.astype(F32) * LOG2E, DEAD)


def update_kernel(
    start,
    at_ref,
    info_ref,
    own_ref,
    other_ref,
    own_bias_ref,
    other_bias_ref,
    wp_ref,
    wo_ref,
    wu_ref,
    wd_ref,
    out_ref,
    sum_s,
    low_s,
    high_s,
):
    _, _, rows, width, chans = own_ref.shape
    count = out_ref.shape[0]
    low_s[...] = jnp.ones_like(low_s)
    high_s[...] = jnp.ones_like(high_s)
    for turn, (from_ref, bias_ref) in enumerate(
        ((own_ref, own_bias_ref), (other_ref, other_bias_ref))
    ):
        update_crop(
            start,
            info_ref[1],
            info_ref[2 + turn],
            info_ref[0] if turn == 0 else 1 - info_ref[0],
            at_ref.at[turn],
            from_ref.at[0],
            from_ref.at[1],
            bias_ref,
            wp_ref,
            wo_ref,
            wu_ref,
            wd_ref,
            out_ref,
            sum_s,
            low_s,
            high_s,
        )


def update_crop(
    start,
    row_base,
    length,
    core,
    at_ref,
    x_ref,
    n_ref,
    bias_ref,
    wp_ref,
    wo_ref,
    wu_ref,
    wd_ref,
    out_ref,
    sum_s,
    low_s,
    high_s,
):
    _, rows, width, chans = x_ref.shape
    heads = bias_ref.shape[0]
    inner = wp_ref.shape[1] // 4
    size_h = inner // heads
    lane = lax.broadcasted_iota(jnp.int32, (width, inner), 1)
    zero = jnp.zeros((), BF16)

    def head_mask(h):
        return (lane >= h * size_h) & (lane < (h + 1) * size_h)

    masks = [head_mask(h) for h in range(heads)]

    def project(block, r):
        proj = jnp.dot(n_ref[block, r], wp_ref[...], preferred_element_type=F32)
        query = (proj[:, :inner] * (size_h ** (-0.5) * LOG2E)).astype(BF16)
        keys = proj[:, inner : 2 * inner].astype(BF16)
        values = proj[:, 2 * inner : 3 * inner].astype(BF16)
        return query, keys, jnp.concatenate([values, jnp.ones_like(values)], 1), proj[:, 3 * inner :]

    def score_of(query, keys, mask, h):
        score = lax.dot_general(jnp.where(mask, query, zero), keys, NT, preferred_element_type=F32)
        return score + bias_ref[h]

    def weigh(score, side):
        return jnp.dot(jnp.exp2(score).astype(BF16), side, preferred_element_type=F32)

    def close(block, first, r, both, gate):
        gated = (jax.nn.sigmoid(gate) * (both[:, :inner] / both[:, inner:])).astype(BF16)
        update = jnp.dot(gated, wo_ref[...], preferred_element_type=F32)
        place = lax.broadcasted_iota(jnp.int32, (width, chans), 0)
        live = (place < length) & (first + r < length)
        middle = x_ref[block, r].astype(F32) + jnp.where(live, update, 0.0)
        return middle.astype(BF16)

    def finish(middle):
        middle = middle.astype(F32)
        normed_mid = normalise(middle).astype(BF16)
        hidden = jnp.dot(normed_mid, wu_ref[...], preferred_element_type=F32)
        hidden = jax.nn.relu(hidden).astype(BF16)
        down = jnp.dot(hidden, wd_ref[...], preferred_element_type=F32)
        return (middle + down).astype(BF16)

    def attend(i, block, first):
        ends = []
        mids = []
        for r in range(rows):
            query, keys, side, gate = project(block, r)
            both = None
            for h in range(heads):
                each = weigh(score_of(query, keys, masks[h], h), side)
                mask = jnp.concatenate([masks[h], masks[h]], 1)
                both = each if both is None else jnp.where(mask, each, both)
            mids.append(close(block, first, r, both, gate))
            ends.append(both[:, inner:])
        out_ref[i, core] = finish(jnp.concatenate(mids, 0)).reshape(rows, width, chans)
        low = functools.reduce(jnp.minimum, ends)
        high = functools.reduce(jnp.maximum, ends)
        low_s[...] = jnp.minimum(low_s[...], jnp.min(low.reshape(-1, 8, inner), 0))
        high_s[...] = jnp.maximum(high_s[...], jnp.max(high.reshape(-1, 8, inner), 0))

    def attend_safe(i, block, first):
        def one_row(r, carry):
            query, keys, side, gate = project(block, r)

            def one_head(h, carry):
                mask = head_mask(h)
                score = score_of(query, keys, mask, h)
                each = weigh(score - jnp.max(score, -1, keepdims=True), side)
                sum_s[...] = jnp.where(jnp.concatenate([mask, mask], 1), each, sum_s[...])
                return carry

            lax.fori_loop(0, heads, one_head, 0)
            out_ref[i, core, r] = finish(close(block, first, r, sum_s[...], gate))
            return carry

        lax.fori_loop(0, rows, one_row, 0)

    count = out_ref.shape[0]

    def one_block(i, carry):
        block = start + i
        first = row_base + at_ref[block] * rows

        @pl.when(first < length)
        def _():
            attend(i, block, first)

        @pl.when(first >= length)
        def _():
            out_ref[i, core] = finish(x_ref[block].reshape(rows * width, chans)).reshape(rows, width, chans)

        return carry

    lax.fori_loop(0, count, one_block, 0, unroll=1)
    good = (jnp.min(low_s[...]) > 1e-20) & (jnp.max(high_s[...]) < 1e30)

    @pl.when(jnp.logical_not(good))
    def _():
        def again(i, carry):
            block = start + i
            first = row_base + at_ref[block] * rows

            @pl.when(first < length)
            def _():
                attend_safe(i, block, first)

            return carry

        lax.fori_loop(0, count, again, 0)


def update_blocks(start, count, at, info, own, other, own_bias, other_bias, weights):
    _, _, rows, width, chans = own.shape
    vmem = pl.BlockSpec(memory_space=pltpu.VMEM)
    smem = pl.BlockSpec(memory_space=pltpu.SMEM)
    inner = weights[0].shape[1] // 4
    work = 4 * rows * width * chans * count * (12 * chans + 4 * width)
    return pl.pallas_call(
        functools.partial(update_kernel, start),
        name="update",
        in_specs=[smem, smem] + [vmem] * 8,
        out_specs=vmem,
        out_shape=jax.ShapeDtypeStruct((count, 2, rows, width, chans), BF16),
        scratch_shapes=[
            pltpu.VMEM((width, 2 * inner), F32),
            pltpu.VMEM((8, inner), F32),
            pltpu.VMEM((8, inner), F32),
        ],
        cost_estimate=pl.CostEstimate(flops=8 * work, bytes_accessed=0, transcendentals=0),
        compiler_params=pltpu.CompilerParams(vmem_limit_bytes=16 * 1024 * 1024),
    )(at, info, own, other, own_bias, other_bias, *weights)


def place_kernel(where_ref, *refs):
    parts, out_ref = refs[:-1], refs[-1]
    for t, part in enumerate(parts):
        out_ref[pl.ds(where_ref[t], 1)] = part[...]


def place_parts(where, parts):
    vmem = pl.BlockSpec(memory_space=pltpu.VMEM)
    count = len(parts)
    return pl.pallas_call(
        place_kernel,
        name="place",
        in_specs=[pl.BlockSpec(memory_space=pltpu.SMEM)] + [vmem] * count,
        out_specs=vmem,
        out_shape=jax.ShapeDtypeStruct((count,) + parts[0].shape[1:], BF16),
        compiler_params=pltpu.CompilerParams(vmem_limit_bytes=16 * 1024 * 1024),
    )(where, *parts)


SHIFTS = [(1, 1), (3, 3), (1, 3), (3, 1), (2, 0), (0, 2), (1, 0), (3, 0), (0, 1), (0, 3)]
SHIFTS += [(2, 1), (2, 3), (1, 2), (3, 2), (2, 2), (0, 0)]


def moved(chip, dx, dy):
    return (chip // 4 + dx) % 4 * 4 + (chip % 4 + dy) % 4


def shards(pair, lengths, block_group, w_proj, w_bias, w_out, w_up, w_down):
    group_idx = lax.axis_index("sample")
    axial_idx = lax.axis_index("axial")
    groups_n = lax.axis_size("sample")
    axial_n = lax.axis_size("axial")
    _, ax_rows, width, chans = pair.shape
    blk_rows = ax_rows // groups_n
    chip, core = group_idx // 2, group_idx % 2
    mate = chip * 2 + 1 - core
    group_ids = jnp.arange(groups_n, dtype=jnp.int32)
    steps = jnp.asarray(SHIFTS, jnp.int32)
    targets = moved(chip, steps[:, 0], steps[:, 1])
    sources = moved(chip, -steps[:, 0], -steps[:, 1]).astype(jnp.int32)

    def found(group, dest):
        row = jnp.take(block_group, group, axis=0)
        return jnp.sum(jnp.where(row[None, :] == dest[:, None], group_ids[None, :], 0), 1)

    keep_at = found(group_idx, targets * 2 + core)
    send_at = found(group_idx, targets * 2 + 1 - core)
    at = jnp.stack([keep_at, found(mate, targets * 2 + core)])
    length, mate_length = jnp.take(lengths, group_idx), jnp.take(lengths, mate)
    info = jnp.stack([core, axial_idx * ax_rows, length, mate_length]).astype(jnp.int32)
    own, send, bias = local_bias(keep_at, send_at, pair[0], w_bias)
    swap = [(g, g ^ 1) for g in range(groups_n)]
    quarters, places = [bias], [axial_idx]
    for d in (2, 1, 3):
        turn = [(a, (a + d) % axial_n) for a in range(axial_n)]
        quarters.append(lax.ppermute(bias, "axial", turn))
        places.append((axial_idx - d) % axial_n)
    other = lax.ppermute(send, "sample", swap)
    crop_bias = join_bias(jnp.stack(places).astype(jnp.int32), quarters)
    other_bias = masked_bias(lax.ppermute(crop_bias, "sample", swap), mate_length)
    own_bias = masked_bias(crop_bias, length)
    weights = (w_proj, w_out, w_up, w_down)
    parts = []
    span = 2
    for start in range(0, len(SHIFTS), span):
        updated = update_blocks(start, span, at, info, own, other, own_bias, other_bias, weights)
        if start >= span:
            before = parts[start - span : start]
            info, updated, before = lax.optimization_barrier((info, updated, before))
            parts[start - span : start] = before
        else:
            info, updated = lax.optimization_barrier((info, updated))
        for t in range(start, start + span):
            part = updated[t - start : t - start + 1]
            dx, dy = SHIFTS[t]
            if dx or dy:
                pairs = [(g, moved(g // 2, dx, dy) * 2 + g % 2) for g in range(groups_n)]
                part = lax.ppermute(part, "sample", pairs)
            parts.append(part)
    out = place_parts(sources, parts)
    return out.reshape(1, 1, groups_n, blk_rows, width, chans)


def solution(mesh):
    return jax.shard_map(
        shards,
        mesh=mesh,
        in_specs=(P("sample", "axial", None, None), P(), P(), P(), P(), P(), P(), P()),
        out_specs=P("sample", "axial", None, None, None, None),
        check_vma=False,
    )
```

```python
import functools

import jax
import jax.numpy as jnp
from jax import lax
from jax.experimental import pallas as pl
from jax.experimental.pallas import tpu as pltpu
from jax.sharding import PartitionSpec as P

F32 = jnp.float32
BF16 = jnp.bfloat16
LOG2E = 1.4426950408889634
DEAD = -1e9
NT = (((1,), (1,)), ((), ()))


def normalise(values_in):
    centre = values_in - jnp.mean(values_in, -1, keepdims=True)
    spread = jnp.mean(centre * centre, -1, keepdims=True)
    return centre * lax.rsqrt(spread + 1e-05)


def bias_kernel(x_hbm, wb_ref, normed_hbm, bias_ref, x_ref, normed_ref, hold_ref, in_sems, out_sems):
    rows = x_ref.shape[0]
    heads = bias_ref.shape[0]
    parts = in_sems.shape[0]
    span = rows // parts

    def fetch(p):
        part = pl.ds(p * span, span)
        return pltpu.make_async_copy(x_hbm.at[part], x_ref.at[part], in_sems.at[p])

    def store(p):
        part = pl.ds(p * span, span)
        return pltpu.make_async_copy(normed_ref.at[part], normed_hbm.at[part], out_sems.at[p])

    for p in range(parts):
        fetch(p).start()
    for p in range(parts):
        fetch(p).wait()
        for r in range(p * span, (p + 1) * span):
            normed = normalise(x_ref[r].astype(F32)).astype(BF16)
            normed_ref[r] = normed
            res = lax.dot_general(wb_ref[...], normed, NT, preferred_element_type=F32)
            for h in range(heads):
                hold_ref[h, r : r + 1, :] = res[h : h + 1]
        store(p).start()
    bias_ref[...] = hold_ref[...].astype(BF16)
    for p in range(parts):
        store(p).wait()


def local_bias(local, w_bias):
    rows, width, chans = local.shape
    heads = w_bias.shape[1]
    wb = jnp.pad(w_bias.T, ((0, 8 - heads), (0, 0)))
    vmem = pl.BlockSpec(memory_space=pltpu.VMEM)
    hbm = pl.BlockSpec(memory_space=pltpu.HBM)
    return pl.pallas_call(
        bias_kernel,
        name="bias",
        in_specs=[hbm, vmem],
        out_specs=[hbm, vmem],
        out_shape=[
            jax.ShapeDtypeStruct((rows, width, chans), BF16),
            jax.ShapeDtypeStruct((heads, rows, width), BF16),
        ],
        scratch_shapes=[
            pltpu.VMEM((rows, width, chans), BF16),
            pltpu.VMEM((rows, width, chans), BF16),
            pltpu.VMEM((heads, rows, width), F32),
            pltpu.SemaphoreType.DMA((8,)),
            pltpu.SemaphoreType.DMA((8,)),
        ],
        compiler_params=pltpu.CompilerParams(vmem_limit_bytes=24 * 1024 * 1024),
    )(local, wb)


def masked_bias(bias, length):
    live = jnp.arange(bias.shape[-1], dtype=jnp.int32) < length
    return jnp.where(live, bias.astype(F32) * LOG2E, DEAD)


def update_kernel(
    groups_ref,
    lengths_ref,
    info_ref,
    x_hbm,
    n_hbm,
    bias_ref,
    wp_ref,
    wo_ref,
    wu_ref,
    wd_ref,
    out_ref,
    order_s,
    x_s,
    n_s,
    mid_s,
    sum_s,
    low_s,
    high_s,
    sems,
):
    count, rows, width, chans = out_ref.shape
    heads = bias_ref.shape[0]
    inner = wp_ref.shape[1] // 4
    size_h = inner // heads
    group = info_ref[0]
    row_base = info_ref[1]
    length = lengths_ref[group]
    lane = lax.broadcasted_iota(jnp.int32, (width, inner), 1)
    zero = jnp.zeros((), BF16)

    for b in range(count):
        order_s[groups_ref[group, b]] = b

    def fetches(i, slot):
        part = order_s[i]
        return (
            pltpu.make_async_copy(x_hbm.at[part], x_s.at[slot], sems.at[0, slot]),
            pltpu.make_async_copy(n_hbm.at[part], n_s.at[slot], sems.at[1, slot]),
        )

    def head_mask(h):
        return (lane >= h * size_h) & (lane < (h + 1) * size_h)

    masks = [head_mask(h) for h in range(heads)]

    def project(normed):
        proj = jnp.dot(normed, wp_ref[...], preferred_element_type=F32)
        query = (proj[:, :inner] * (size_h ** (-0.5) * LOG2E)).astype(BF16)
        keys = proj[:, inner : 2 * inner].astype(BF16)
        values = proj[:, 2 * inner : 3 * inner].astype(BF16)
        return query, keys, jnp.concatenate([values, jnp.ones_like(values)], 1), proj[:, 3 * inner :]

    def score_of(query, keys, mask, h):
        score = lax.dot_general(jnp.where(mask, query, zero), keys, NT, preferred_element_type=F32)
        return score + bias_ref[h]

    def weigh(score, side):
        return jnp.dot(jnp.exp2(score).astype(BF16), side, preferred_element_type=F32)

    def gated_of(both, gate):
        return (jax.nn.sigmoid(gate) * (both[:, :inner] / both[:, inner:])).astype(BF16)

    def close(before, first, gated):
        update = jnp.dot(gated, wo_ref[...], preferred_element_type=F32)
        place = lax.broadcasted_iota(jnp.int32, update.shape, 0)
        live = (place % width < length) & (first + place // width < length)
        middle = before.astype(F32) + jnp.where(live, update, 0.0)
        return middle.astype(BF16)

    def finish(middle):
        middle = middle.astype(F32)
        normed_mid = normalise(middle).astype(BF16)
        hidden = jnp.dot(normed_mid, wu_ref[...], preferred_element_type=F32)
        hidden = jax.nn.relu(hidden).astype(BF16)
        down = jnp.dot(hidden, wd_ref[...], preferred_element_type=F32)
        return (middle + down).astype(BF16)

    def store(i, updated):
        out_ref[i] = updated.reshape(rows, width, chans)

    def attend(i, slot, first):
        past = mid_s[...]
        query, keys, side, gate = project(n_s[slot].reshape(rows * width, chans))
        ends = []
        for r in range(rows):
            at = slice(r * width, (r + 1) * width)
            both = None
            for h in range(heads):
                each = weigh(score_of(query[at], keys[at], masks[h], h), side[at])
                mask = jnp.concatenate([masks[h], masks[h]], 1)
                both = each if both is None else jnp.where(mask, each, both)
            ends.append(both)
        gated = gated_of(jnp.concatenate(ends, 0), gate)
        store(jnp.maximum(i - 1, 0), finish(past))
        mid_s[...] = close(x_s[slot].reshape(rows * width, chans), first, gated)
        low = functools.reduce(jnp.minimum, [e[:, inner:] for e in ends])
        high = functools.reduce(jnp.maximum, [e[:, inner:] for e in ends])
        low_s[...] = jnp.minimum(low_s[...], jnp.min(low.reshape(-1, 8, inner), 0))
        high_s[...] = jnp.maximum(high_s[...], jnp.max(high.reshape(-1, 8, inner), 0))

    low_s[...] = jnp.ones_like(low_s)
    high_s[...] = jnp.ones_like(high_s)
    mid_s[...] = jnp.zeros_like(mid_s)
    for copy in fetches(0, 0):
        copy.start()

    def one_block(i, carry):
        slot = lax.rem(i, 2)
        first = row_base + order_s[i] * rows

        @pl.when(i + 1 < count)
        def _():
            for copy in fetches(i + 1, 1 - slot):
                copy.start()

        for copy in fetches(i, slot):
            copy.wait()

        @pl.when(first < length)
        def _():
            attend(i, slot, first)

        @pl.when(first >= length)
        def _():
            store(jnp.maximum(i - 1, 0), finish(mid_s[...]))
            mid_s[...] = x_s[slot].reshape(rows * width, chans)

        return carry

    lax.fori_loop(0, count, one_block, 0)
    store(count - 1, finish(mid_s[...]))
    good = (jnp.min(low_s[...]) > 1e-20) & (jnp.max(high_s[...]) < 1e30)

    @pl.when(jnp.logical_not(good))
    def _():
        def again(i, carry):
            first = row_base + order_s[i] * rows

            @pl.when(first < length)
            def _():
                for copy in fetches(i, 0):
                    copy.start()
                for copy in fetches(i, 0):
                    copy.wait()

                def one_row(r, carry):
                    query, keys, side, gate = project(n_s[0, r])

                    def one_head(h, carry):
                        mask = head_mask(h)
                        score = score_of(query, keys, mask, h)
                        each = weigh(score - jnp.max(score, -1, keepdims=True), side)
                        sum_s[...] = jnp.where(jnp.concatenate([mask, mask], 1), each, sum_s[...])
                        return carry

                    lax.fori_loop(0, heads, one_head, 0)
                    gated = gated_of(sum_s[...], gate)
                    out_ref[i, r] = finish(close(x_s[0, r], first + r, gated))
                    return carry

                lax.fori_loop(0, rows, one_row, 0)

            return carry

        lax.fori_loop(0, count, again, 0)


def update_blocks(groups, lengths, info, blocks, normeds, bias, w_proj, w_out, w_up, w_down):
    count, rows, width, chans = blocks.shape
    inner = w_proj.shape[1] // 4
    vmem = pl.BlockSpec(memory_space=pltpu.VMEM)
    smem = pl.BlockSpec(memory_space=pltpu.SMEM)
    hbm = pl.BlockSpec(memory_space=pltpu.HBM)
    return pl.pallas_call(
        update_kernel,
        name="update",
        in_specs=[smem, smem, smem, hbm, hbm] + [vmem] * 5,
        out_specs=vmem,
        out_shape=jax.ShapeDtypeStruct((count, rows, width, chans), BF16),
        scratch_shapes=[
            pltpu.SMEM((count,), jnp.int32),
            pltpu.VMEM((2, rows, width, chans), BF16),
            pltpu.VMEM((2, rows, width, chans), BF16),
            pltpu.VMEM((rows * width, chans), BF16),
            pltpu.VMEM((width, 2 * inner), F32),
            pltpu.VMEM((8, inner), F32),
            pltpu.VMEM((8, inner), F32),
            pltpu.SemaphoreType.DMA((2, 2)),
        ],
        compiler_params=pltpu.CompilerParams(vmem_limit_bytes=24 * 1024 * 1024),
    )(groups, lengths, info, blocks, normeds, bias, w_proj, w_out, w_up, w_down)


def shards(pair, lengths, block_group, w_proj, w_bias, w_out, w_up, w_down):
    group_idx = lax.axis_index("sample")
    axial_idx = lax.axis_index("axial")
    groups_n = lax.axis_size("sample")
    _, ax_rows, width, chans = pair.shape
    blk_rows = ax_rows // groups_n
    local = pair[0]
    info = jnp.stack([group_idx, axial_idx * ax_rows]).astype(jnp.int32)
    normed, bias = local_bias(local, w_bias)
    length = jnp.take(lengths, group_idx)
    crop_bias = masked_bias(lax.all_gather(bias, "axial", axis=1, tiled=True), length)
    shape = (groups_n, blk_rows, width, chans)
    updated = update_blocks(
        block_group,
        lengths,
        info,
        local.reshape(shape),
        normed.reshape(shape),
        crop_bias,
        w_proj,
        w_out,
        w_up,
        w_down,
    )
    arrived = lax.all_to_all(updated, "sample", split_axis=0, concat_axis=0, tiled=True)
    return arrived.reshape(1, 1, groups_n, blk_rows, width, chans)


def solution(mesh):
    return jax.shard_map(
        shards,
        mesh=mesh,
        in_specs=(P("sample", "axial", None, None), P(), P(), P(), P(), P(), P(), P()),
        out_specs=P("sample", "axial", None, None, None, None),
        check_vma=False,
    )
```

```python
import functools

import jax
import jax.numpy as jnp
from jax import lax
from jax.experimental import pallas as pl
from jax.experimental.pallas import tpu as pltpu
from jax.sharding import PartitionSpec as P

F32 = jnp.float32
BF16 = jnp.bfloat16
LOG2E = 1.4426950408889634
DEAD = -1e9
NT = (((1,), (1,)), ((), ()))


def normalise(values_in):
    centre = values_in - jnp.mean(values_in, -1, keepdims=True)
    spread = jnp.mean(centre * centre, -1, keepdims=True)
    return centre * lax.rsqrt(spread + 1e-05)


def bias_kernel(x_hbm, wb_ref, normed_hbm, bias_ref, x_ref, normed_ref, hold_ref, in_sems, out_sems):
    rows = x_ref.shape[0]
    heads = bias_ref.shape[0]
    parts = in_sems.shape[0]
    span = rows // parts

    def fetch(p):
        part = pl.ds(p * span, span)
        return pltpu.make_async_copy(x_hbm.at[part], x_ref.at[part], in_sems.at[p])

    def store(p):
        part = pl.ds(p * span, span)
        return pltpu.make_async_copy(normed_ref.at[part], normed_hbm.at[part], out_sems.at[p])

    for p in range(parts):
        fetch(p).start()
    for p in range(parts):
        fetch(p).wait()
        for r in range(p * span, (p + 1) * span):
            normed = normalise(x_ref[r].astype(F32)).astype(BF16)
            normed_ref[r] = normed
            res = lax.dot_general(wb_ref[...], normed, NT, preferred_element_type=F32)
            for h in range(heads):
                hold_ref[h, r : r + 1, :] = res[h : h + 1]
        store(p).start()
    bias_ref[...] = hold_ref[...].astype(BF16)
    for p in range(parts):
        store(p).wait()


def local_bias(local, w_bias):
    rows, width, chans = local.shape
    heads = w_bias.shape[1]
    wb = jnp.pad(w_bias.T, ((0, 8 - heads), (0, 0)))
    vmem = pl.BlockSpec(memory_space=pltpu.VMEM)
    hbm = pl.BlockSpec(memory_space=pltpu.HBM)
    return pl.pallas_call(
        bias_kernel,
        name="bias",
        in_specs=[hbm, vmem],
        out_specs=[hbm, vmem],
        out_shape=[
            jax.ShapeDtypeStruct((rows, width, chans), BF16),
            jax.ShapeDtypeStruct((heads, rows, width), BF16),
        ],
        scratch_shapes=[
            pltpu.VMEM((rows, width, chans), BF16),
            pltpu.VMEM((rows, width, chans), BF16),
            pltpu.VMEM((heads, rows, width), F32),
            pltpu.SemaphoreType.DMA((8,)),
            pltpu.SemaphoreType.DMA((8,)),
        ],
        compiler_params=pltpu.CompilerParams(vmem_limit_bytes=61 * 1024 * 1024),
    )(local, wb)


def update_kernel(
    groups_ref,
    lengths_ref,
    info_ref,
    x_hbm,
    n_hbm,
    bias_ref,
    wp_ref,
    wo_ref,
    wu_ref,
    wd_ref,
    out_ref,
    order_s,
    bias_s,
    x_s,
    n_s,
    mid_s,
    sum_s,
    low_s,
    high_s,
    sems,
):
    count, rows, width, chans = out_ref.shape
    per = x_s.shape[1]
    steps = count // per
    span = per * rows * width
    heads = bias_ref.shape[0]
    inner = wp_ref.shape[1] // 4
    size_h = inner // heads
    group = info_ref[0]
    row_base = info_ref[1]
    length = lengths_ref[group]
    lane = lax.broadcasted_iota(jnp.int32, (width, inner), 1)
    zero = jnp.zeros((), BF16)

    keys_live = lax.broadcasted_iota(jnp.int32, (width, width), 1) < length

    for b in range(count):
        order_s[groups_ref[group, b]] = b

    def fetches(i, slot):
        copies = []
        for p in range(per):
            part = order_s[i * per + p]
            copies += [
                pltpu.make_async_copy(x_hbm.at[part], x_s.at[slot, p], sems.at[0, p, slot]),
                pltpu.make_async_copy(n_hbm.at[part], n_s.at[slot, p], sems.at[1, p, slot]),
            ]
        return copies

    def firsts(i):
        return [row_base + order_s[i * per + p] * rows for p in range(per)]

    def head_mask(h):
        return (lane >= h * size_h) & (lane < (h + 1) * size_h)

    masks = [head_mask(h) for h in range(heads)]

    def project(normed):
        proj = jnp.dot(normed, wp_ref[...], preferred_element_type=F32)
        query = (proj[:, :inner] * (size_h ** (-0.5) * LOG2E)).astype(BF16)
        keys = proj[:, inner : 2 * inner].astype(BF16)
        values = proj[:, 2 * inner : 3 * inner].astype(BF16)
        return query, keys, jnp.concatenate([values, jnp.ones_like(values)], 1), proj[:, 3 * inner :]

    def score_of(query, keys, mask, h):
        score = lax.dot_general(jnp.where(mask, query, zero), keys, NT, preferred_element_type=F32)
        return score + bias_s[h]

    def weigh(score, side):
        return jnp.dot(jnp.exp2(score).astype(BF16), side, preferred_element_type=F32)

    def gated_of(both, gate):
        return (jax.nn.sigmoid(gate) * (both[:, :inner] / both[:, inner:])).astype(BF16)

    def close(before, first, gated):
        update = jnp.dot(gated, wo_ref[...], preferred_element_type=F32)
        made = []
        for r, row in enumerate(first):
            at = slice(r * width, (r + 1) * width)
            place = lax.broadcasted_iota(jnp.int32, (width, chans), 0)
            live = (place < length) & (row < length)
            middle = before[at].astype(F32) + jnp.where(live, update[at], 0.0)
            made.append(middle.astype(BF16))
        return jnp.concatenate(made, 0)

    def finish(middle):
        middle = middle.astype(F32)
        normed_mid = normalise(middle).astype(BF16)
        hidden = jnp.dot(normed_mid, wu_ref[...], preferred_element_type=F32)
        hidden = jax.nn.relu(hidden).astype(BF16)
        down = jnp.dot(hidden, wd_ref[...], preferred_element_type=F32)
        return (middle + down).astype(BF16)

    def store(i, updated):
        out_ref[pl.ds(i * per, per)] = updated.reshape(per, rows, width, chans)

    def attend(i, slot, first):
        past = mid_s[...]
        query, keys, side, gate = project(n_s[slot].reshape(span, chans))
        ends = []
        for r in range(per * rows):
            at = slice(r * width, (r + 1) * width)
            both = None
            for h in range(heads):
                each = weigh(score_of(query[at], keys[at], masks[h], h), side[at])
                mask = jnp.concatenate([masks[h], masks[h]], 1)
                both = each if both is None else jnp.where(mask, each, both)
            ends.append(both)
        gated = gated_of(jnp.concatenate(ends, 0), gate)
        store(jnp.maximum(i - 1, 0), finish(past))
        mid_s[...] = close(
            x_s[slot].reshape(span, chans), [f + r for f in first for r in range(rows)], gated
        )
        low = functools.reduce(jnp.minimum, [e[:, inner:] for e in ends])
        high = functools.reduce(jnp.maximum, [e[:, inner:] for e in ends])
        low_s[...] = jnp.minimum(low_s[...], jnp.min(low.reshape(-1, 8, inner), 0))
        high_s[...] = jnp.maximum(high_s[...], jnp.max(high.reshape(-1, 8, inner), 0))

    for copy in fetches(0, 0):
        copy.start()
    for h in range(heads):
        bias_s[h] = jnp.where(keys_live, bias_ref[h].astype(F32) * LOG2E, DEAD)
    low_s[...] = jnp.ones_like(low_s)
    high_s[...] = jnp.ones_like(high_s)
    mid_s[...] = jnp.zeros_like(mid_s)
    def one_block(i, carry):
        slot = lax.rem(i, 2)
        first = firsts(i)
        some = functools.reduce(jnp.minimum, first) < length

        @pl.when(i + 1 < steps)
        def _():
            for copy in fetches(i + 1, 1 - slot):
                copy.start()

        for copy in fetches(i, slot):
            copy.wait()

        @pl.when(some)
        def _():
            attend(i, slot, first)

        @pl.when(jnp.logical_not(some))
        def _():
            store(jnp.maximum(i - 1, 0), finish(mid_s[...]))
            mid_s[...] = x_s[slot].reshape(span, chans)

        return carry

    lax.fori_loop(0, steps, one_block, 0)
    store(steps - 1, finish(mid_s[...]))
    good = (jnp.min(low_s[...]) > 1e-20) & (jnp.max(high_s[...]) < 1e30)

    @pl.when(jnp.logical_not(good))
    def _():
        def again(i, carry):
            for copy in fetches(i, 0):
                copy.start()
            for copy in fetches(i, 0):
                copy.wait()

            def one_row(r, carry):
                p = r // rows
                row = row_base + order_s[i * per + p] * rows + lax.rem(r, rows)
                query, keys, side, gate = project(n_s[0, p, lax.rem(r, rows)])

                def one_head(h, carry):
                    mask = head_mask(h)
                    score = score_of(query, keys, mask, h)
                    each = weigh(score - jnp.max(score, -1, keepdims=True), side)
                    sum_s[...] = jnp.where(jnp.concatenate([mask, mask], 1), each, sum_s[...])
                    return carry

                lax.fori_loop(0, heads, one_head, 0)
                gated = gated_of(sum_s[...], gate)
                middle = close(x_s[0, p, lax.rem(r, rows)], [row], gated)
                out_ref[i * per + p, lax.rem(r, rows)] = finish(middle)
                return carry

            lax.fori_loop(0, per * rows, one_row, 0)
            return carry

        lax.fori_loop(0, steps, again, 0)


def update_blocks(groups, lengths, info, blocks, normeds, bias, w_proj, w_out, w_up, w_down):
    count, rows, width, chans = blocks.shape
    inner = w_proj.shape[1] // 4
    per = 2
    vmem = pl.BlockSpec(memory_space=pltpu.VMEM)
    smem = pl.BlockSpec(memory_space=pltpu.SMEM)
    hbm = pl.BlockSpec(memory_space=pltpu.HBM)
    return pl.pallas_call(
        update_kernel,
        name="update",
        in_specs=[smem, smem, smem, hbm, hbm] + [vmem] * 5,
        out_specs=vmem,
        out_shape=jax.ShapeDtypeStruct((count, rows, width, chans), BF16),
        scratch_shapes=[
            pltpu.SMEM((count,), jnp.int32),
            pltpu.VMEM(bias.shape, F32),
            pltpu.VMEM((2, per, rows, width, chans), BF16),
            pltpu.VMEM((2, per, rows, width, chans), BF16),
            pltpu.VMEM((per * rows * width, chans), BF16),
            pltpu.VMEM((width, 2 * inner), F32),
            pltpu.VMEM((8, inner), F32),
            pltpu.VMEM((8, inner), F32),
            pltpu.SemaphoreType.DMA((2, per, 2)),
        ],
        compiler_params=pltpu.CompilerParams(vmem_limit_bytes=56 * 1024 * 1024),
    )(groups, lengths, info, blocks, normeds, bias, w_proj, w_out, w_up, w_down)


def shards(pair, lengths, block_group, w_proj, w_bias, w_out, w_up, w_down):
    group_idx = lax.axis_index("sample")
    axial_idx = lax.axis_index("axial")
    groups_n = lax.axis_size("sample")
    _, ax_rows, width, chans = pair.shape
    blk_rows = ax_rows // groups_n
    local = pair[0]
    info = jnp.stack([group_idx, axial_idx * ax_rows]).astype(jnp.int32)
    normed, bias = local_bias(local, w_bias)
    crop_bias = lax.all_gather(bias, "axial", axis=1, tiled=True)
    shape = (groups_n, blk_rows, width, chans)
    updated = update_blocks(
        block_group,
        lengths,
        info,
        local.reshape(shape),
        normed.reshape(shape),
        crop_bias,
        w_proj,
        w_out,
        w_up,
        w_down,
    )
    arrived = lax.all_to_all(updated, "sample", split_axis=0, concat_axis=0, tiled=True)
    return arrived.reshape(1, 1, groups_n, blk_rows, width, chans)


def solution(mesh):
    return jax.shard_map(
        shards,
        mesh=mesh,
        in_specs=(P("sample", "axial", None, None), P(), P(), P(), P(), P(), P(), P()),
        out_specs=P("sample", "axial", None, None, None, None),
        check_vma=False,
    )
```

```python
import functools

import jax
import jax.numpy as jnp
from jax import lax
from jax.experimental import pallas as pl
from jax.experimental.pallas import tpu as pltpu
from jax.sharding import PartitionSpec as P

F32 = jnp.float32
BF16 = jnp.bfloat16
LOG2E = 1.4426950408889634
DEAD = -1e9
NT = (((1,), (1,)), ((), ()))


def normalise(values_in):
    centre = values_in - jnp.mean(values_in, -1, keepdims=True)
    spread = jnp.mean(centre * centre, -1, keepdims=True)
    return centre * lax.rsqrt(spread + 1e-05)


def bias_kernel(x_hbm, wb_ref, normed_hbm, bias_ref, x_ref, normed_ref, hold_ref, in_sems, out_sems):
    rows = x_ref.shape[0]
    heads = bias_ref.shape[0]
    parts = in_sems.shape[0]
    span = rows // parts

    def fetch(p):
        part = pl.ds(p * span, span)
        return pltpu.make_async_copy(x_hbm.at[part], x_ref.at[part], in_sems.at[p])

    def store(p):
        part = pl.ds(p * span, span)
        return pltpu.make_async_copy(normed_ref.at[part], normed_hbm.at[part], out_sems.at[p])

    for p in range(parts):
        fetch(p).start()

    def one_part(p, carry):
        fetch(p).wait()
        for r in range(span):
            row = p * span + r
            normed = normalise(x_ref[row].astype(F32)).astype(BF16)
            normed_ref[row] = normed
            res = lax.dot_general(wb_ref[...], normed, NT, preferred_element_type=F32)
            for h in range(heads):
                hold_ref[p, h, r : r + 1, :] = res[h : h + 1]
        store(p).start()
        return carry

    lax.fori_loop(0, parts, one_part, 0)
    for p in range(0, parts, 2):
        pair = jnp.concatenate([hold_ref[p], hold_ref[p + 1]], 1)
        bias_ref[:, p * span : (p + 2) * span, :] = pair.astype(BF16)
    for p in range(parts):
        store(p).wait()


def local_bias(local, w_bias):
    rows, width, chans = local.shape
    heads = w_bias.shape[1]
    wb = jnp.pad(w_bias.T, ((0, 8 - heads), (0, 0)))
    vmem = pl.BlockSpec(memory_space=pltpu.VMEM)
    hbm = pl.BlockSpec(memory_space=pltpu.HBM)
    return pl.pallas_call(
        bias_kernel,
        name="bias",
        in_specs=[hbm, vmem],
        out_specs=[hbm, vmem],
        out_shape=[
            jax.ShapeDtypeStruct((rows, width, chans), BF16),
            jax.ShapeDtypeStruct((heads, rows, width), BF16),
        ],
        scratch_shapes=[
            pltpu.VMEM((rows, width, chans), BF16),
            pltpu.VMEM((rows, width, chans), BF16),
            pltpu.VMEM((8, heads, rows // 8, width), F32),
            pltpu.SemaphoreType.DMA((8,)),
            pltpu.SemaphoreType.DMA((8,)),
        ],
        compiler_params=pltpu.CompilerParams(vmem_limit_bytes=61 * 1024 * 1024),
    )(local, wb)


def update_kernel(
    groups_ref,
    lengths_ref,
    info_ref,
    x_hbm,
    n_hbm,
    bias_ref,
    wp_ref,
    wo_ref,
    wu_ref,
    wd_ref,
    out_ref,
    order_s,
    bias_s,
    x_s,
    n_s,
    mid_s,
    sum_s,
    low_s,
    high_s,
    sems,
):
    count, rows, width, chans = out_ref.shape
    per = x_s.shape[1]
    steps = count // per
    span = per * rows * width
    heads = bias_ref.shape[0]
    inner = wp_ref.shape[1] // 4
    size_h = inner // heads
    group = info_ref[0]
    row_base = info_ref[1]
    length = lengths_ref[group]
    lane = lax.broadcasted_iota(jnp.int32, (width, inner), 1)
    zero = jnp.zeros((), BF16)

    keys_live = lax.broadcasted_iota(jnp.int32, (width, width), 1) < length

    for b in range(count):
        order_s[groups_ref[group, b]] = b

    def fetches(i, slot):
        copies = []
        for p in range(per):
            part = order_s[i * per + p]
            copies += [
                pltpu.make_async_copy(x_hbm.at[part], x_s.at[slot, p], sems.at[0, p, slot]),
                pltpu.make_async_copy(n_hbm.at[part], n_s.at[slot, p], sems.at[1, p, slot]),
            ]
        return copies

    def firsts(i):
        return [row_base + order_s[i * per + p] * rows for p in range(per)]

    def head_mask(h):
        return (lane >= h * size_h) & (lane < (h + 1) * size_h)

    masks = [head_mask(h) for h in range(heads)]

    def project(normed):
        proj = jnp.dot(normed, wp_ref[...], preferred_element_type=F32)
        query = (proj[:, :inner] * size_h ** (-0.5)).astype(BF16)
        keys = proj[:, inner : 2 * inner].astype(BF16)
        values = proj[:, 2 * inner : 3 * inner].astype(BF16)
        return query, keys, jnp.concatenate([values, jnp.ones_like(values)], 1), proj[:, 3 * inner :]

    def score_of(query, keys, mask, h):
        score = lax.dot_general(jnp.where(mask, query, zero), keys, NT, preferred_element_type=F32)
        return score * LOG2E + bias_s[h]

    def weigh(score, side):
        return jnp.dot(jnp.exp2(score).astype(BF16), side, preferred_element_type=F32)

    def gated_of(both, gate):
        return (jax.nn.sigmoid(gate) * (both[:, :inner] / both[:, inner:])).astype(BF16)

    def close(before, first, gated):
        update = jnp.dot(gated, wo_ref[...], preferred_element_type=F32)
        made = []
        for r, row in enumerate(first):
            at = slice(r * width, (r + 1) * width)
            place = lax.broadcasted_iota(jnp.int32, (width, chans), 0)
            live = (place < length) & (row < length)
            middle = before[at].astype(F32) + jnp.where(live, update[at], 0.0)
            made.append(middle.astype(BF16))
        return jnp.concatenate(made, 0)

    def finish(middle):
        middle = middle.astype(F32)
        normed_mid = normalise(middle).astype(BF16)
        hidden = jnp.dot(normed_mid, wu_ref[...], preferred_element_type=F32)
        hidden = jax.nn.relu(hidden).astype(BF16)
        down = jnp.dot(hidden, wd_ref[...], preferred_element_type=F32)
        return (middle + down).astype(BF16)

    def store(i, updated):
        out_ref[pl.ds(i * per, per)] = updated.reshape(per, rows, width, chans)

    def attend(i, slot, first):
        past = mid_s[...]
        query, keys, side, gate = project(n_s[slot].reshape(span, chans))
        ends = []
        for r in range(per * rows):
            at = slice(r * width, (r + 1) * width)
            both = None
            for h in range(heads):
                each = weigh(score_of(query[at], keys[at], masks[h], h), side[at])
                mask = jnp.concatenate([masks[h], masks[h]], 1)
                both = each if both is None else jnp.where(mask, each, both)
            ends.append(both)
        gated = gated_of(jnp.concatenate(ends, 0), gate)
        store(jnp.maximum(i - 1, 0), finish(past))
        mid_s[...] = close(
            x_s[slot].reshape(span, chans), [f + r for f in first for r in range(rows)], gated
        )
        low = functools.reduce(jnp.minimum, [e[:, inner:] for e in ends])
        high = functools.reduce(jnp.maximum, [e[:, inner:] for e in ends])
        low_s[...] = jnp.minimum(low_s[...], jnp.min(low.reshape(-1, 8, inner), 0))
        high_s[...] = jnp.maximum(high_s[...], jnp.max(high.reshape(-1, 8, inner), 0))

    for copy in fetches(0, 0):
        copy.start()
    for h in range(heads):
        bias_s[h] = jnp.where(keys_live, bias_ref[h].astype(F32) * LOG2E, DEAD)
    low_s[...] = jnp.ones_like(low_s)
    high_s[...] = jnp.ones_like(high_s)
    mid_s[...] = jnp.zeros_like(mid_s)
    def one_block(i, carry):
        slot = lax.rem(i, 2)
        first = firsts(i)
        some = functools.reduce(jnp.minimum, first) < length

        @pl.when(i + 1 < steps)
        def _():
            for copy in fetches(i + 1, 1 - slot):
                copy.start()

        for copy in fetches(i, slot):
            copy.wait()

        @pl.when(some)
        def _():
            attend(i, slot, first)

        @pl.when(jnp.logical_not(some))
        def _():
            store(jnp.maximum(i - 1, 0), finish(mid_s[...]))
            mid_s[...] = x_s[slot].reshape(span, chans)

        return carry

    lax.fori_loop(0, steps, one_block, 0)
    store(steps - 1, finish(mid_s[...]))
    good = (jnp.min(low_s[...]) > 1e-20) & (jnp.max(high_s[...]) < 1e30)

    @pl.when(jnp.logical_not(good))
    def _():
        def again(i, carry):
            for copy in fetches(i, 0):
                copy.start()
            for copy in fetches(i, 0):
                copy.wait()

            def one_row(r, carry):
                p = r // rows
                row = row_base + order_s[i * per + p] * rows + lax.rem(r, rows)
                query, keys, side, gate = project(n_s[0, p, lax.rem(r, rows)])

                def one_head(h, carry):
                    mask = head_mask(h)
                    score = score_of(query, keys, mask, h)
                    each = weigh(score - jnp.max(score, -1, keepdims=True), side)
                    sum_s[...] = jnp.where(jnp.concatenate([mask, mask], 1), each, sum_s[...])
                    return carry

                lax.fori_loop(0, heads, one_head, 0)
                gated = gated_of(sum_s[...], gate)
                middle = close(x_s[0, p, lax.rem(r, rows)], [row], gated)
                out_ref[i * per + p, lax.rem(r, rows)] = finish(middle)
                return carry

            lax.fori_loop(0, per * rows, one_row, 0)
            return carry

        lax.fori_loop(0, steps, again, 0)


def update_blocks(groups, lengths, info, blocks, normeds, bias, w_proj, w_out, w_up, w_down):
    count, rows, width, chans = blocks.shape
    inner = w_proj.shape[1] // 4
    per = 2
    vmem = pl.BlockSpec(memory_space=pltpu.VMEM)
    smem = pl.BlockSpec(memory_space=pltpu.SMEM)
    hbm = pl.BlockSpec(memory_space=pltpu.HBM)
    return pl.pallas_call(
        update_kernel,
        name="update",
        in_specs=[smem, smem, smem, hbm, hbm] + [vmem] * 5,
        out_specs=vmem,
        out_shape=jax.ShapeDtypeStruct((count, rows, width, chans), BF16),
        scratch_shapes=[
            pltpu.SMEM((count,), jnp.int32),
            pltpu.VMEM(bias.shape, F32),
            pltpu.VMEM((2, per, rows, width, chans), BF16),
            pltpu.VMEM((2, per, rows, width, chans), BF16),
            pltpu.VMEM((per * rows * width, chans), BF16),
            pltpu.VMEM((width, 2 * inner), F32),
            pltpu.VMEM((8, inner), F32),
            pltpu.VMEM((8, inner), F32),
            pltpu.SemaphoreType.DMA((2, per, 2)),
        ],
        compiler_params=pltpu.CompilerParams(vmem_limit_bytes=56 * 1024 * 1024),
    )(groups, lengths, info, blocks, normeds, bias, w_proj, w_out, w_up, w_down)


def shards(pair, lengths, block_group, w_proj, w_bias, w_out, w_up, w_down):
    group_idx = lax.axis_index("sample")
    axial_idx = lax.axis_index("axial")
    groups_n = lax.axis_size("sample")
    _, ax_rows, width, chans = pair.shape
    blk_rows = ax_rows // groups_n
    local = pair[0]
    info = jnp.stack([group_idx, axial_idx * ax_rows]).astype(jnp.int32)
    normed, bias = local_bias(local, w_bias)
    crop_bias = lax.all_gather(bias, "axial", axis=1, tiled=True)
    shape = (groups_n, blk_rows, width, chans)
    updated = update_blocks(
        block_group,
        lengths,
        info,
        local.reshape(shape),
        normed.reshape(shape),
        crop_bias,
        w_proj,
        w_out,
        w_up,
        w_down,
    )
    arrived = lax.all_to_all(updated, "sample", split_axis=0, concat_axis=0, tiled=True)
    return arrived.reshape(1, 1, groups_n, blk_rows, width, chans)


def solution(mesh):
    return jax.shard_map(
        shards,
        mesh=mesh,
        in_specs=(P("sample", "axial", None, None), P(), P(), P(), P(), P(), P(), P()),
        out_specs=P("sample", "axial", None, None, None, None),
        check_vma=False,
    )
```

```python
import functools

import jax
import jax.numpy as jnp
from jax import lax
from jax.experimental import pallas as pl
from jax.experimental.pallas import tpu as pltpu
from jax.sharding import PartitionSpec as P

F32 = jnp.float32
BF16 = jnp.bfloat16
LOG2E = 1.4426950408889634
DEAD = -1e9
NT = (((1,), (1,)), ((), ()))


def normalise(values_in):
    centre = values_in - jnp.mean(values_in, -1, keepdims=True)
    spread = jnp.mean(centre * centre, -1, keepdims=True)
    return centre * lax.rsqrt(spread + 1e-05)


def bias_kernel(x_hbm, wb_ref, normed_hbm, bias_ref, x_ref, normed_ref, hold_ref, in_sems, out_sems):
    rows = x_ref.shape[0]
    heads = bias_ref.shape[0]
    parts = in_sems.shape[0]
    span = rows // parts

    def fetch(p):
        part = pl.ds(p * span, span)
        return pltpu.make_async_copy(x_hbm.at[part], x_ref.at[part], in_sems.at[p])

    def store(p):
        part = pl.ds(p * span, span)
        return pltpu.make_async_copy(normed_ref.at[part], normed_hbm.at[part], out_sems.at[p])

    ahead = 2
    for p in range(ahead):
        fetch(p).start()

    def one_part(p, carry):
        @pl.when(p + ahead < parts)
        def _():
            fetch(p + ahead).start()

        fetch(p).wait()
        for r in range(span):
            row = p * span + r
            normed = normalise(x_ref[row].astype(F32)).astype(BF16)
            normed_ref[row] = normed
            res = lax.dot_general(wb_ref[...], normed, NT, preferred_element_type=F32)
            for h in range(heads):
                hold_ref[p, h, r : r + 1, :] = res[h : h + 1]
        store(p).start()
        return carry

    lax.fori_loop(0, parts, one_part, 0)
    for p in range(0, parts, 2):
        pair = jnp.concatenate([hold_ref[p], hold_ref[p + 1]], 1)
        bias_ref[:, p * span : (p + 2) * span, :] = pair.astype(BF16)
    for p in range(parts):
        store(p).wait()


def local_bias(local, w_bias):
    rows, width, chans = local.shape
    heads = w_bias.shape[1]
    wb = jnp.pad(w_bias.T, ((0, 8 - heads), (0, 0)))
    vmem = pl.BlockSpec(memory_space=pltpu.VMEM)
    hbm = pl.BlockSpec(memory_space=pltpu.HBM)
    return pl.pallas_call(
        bias_kernel,
        name="bias",
        in_specs=[hbm, vmem],
        out_specs=[hbm, vmem],
        out_shape=[
            jax.ShapeDtypeStruct((rows, width, chans), BF16),
            jax.ShapeDtypeStruct((heads, rows, width), BF16),
        ],
        scratch_shapes=[
            pltpu.VMEM((rows, width, chans), BF16),
            pltpu.VMEM((rows, width, chans), BF16),
            pltpu.VMEM((8, heads, rows // 8, width), F32),
            pltpu.SemaphoreType.DMA((8,)),
            pltpu.SemaphoreType.DMA((8,)),
        ],
        compiler_params=pltpu.CompilerParams(vmem_limit_bytes=61 * 1024 * 1024),
    )(local, wb)


def update_kernel(
    groups_ref,
    lengths_ref,
    info_ref,
    x_hbm,
    n_hbm,
    bias_ref,
    wp_ref,
    wo_ref,
    wu_ref,
    wd_ref,
    out_ref,
    order_s,
    bias_s,
    x_s,
    n_s,
    mid_s,
    sum_s,
    low_s,
    high_s,
    sems,
):
    count, rows, width, chans = out_ref.shape
    per = x_s.shape[1]
    steps = count // per
    span = per * rows * width
    heads = bias_ref.shape[0]
    inner = wp_ref.shape[1] // 4
    size_h = inner // heads
    group = info_ref[0]
    row_base = info_ref[1]
    length = lengths_ref[group]
    lane = lax.broadcasted_iota(jnp.int32, (width, inner), 1)
    zero = jnp.zeros((), BF16)

    keys_live = lax.broadcasted_iota(jnp.int32, (width, width), 1) < length

    for b in range(count):
        order_s[groups_ref[group, b]] = b

    def fetches(i, slot):
        copies = []
        for p in range(per):
            part = order_s[i * per + p]
            copies += [
                pltpu.make_async_copy(x_hbm.at[part], x_s.at[slot, p], sems.at[0, p, slot]),
                pltpu.make_async_copy(n_hbm.at[part], n_s.at[slot, p], sems.at[1, p, slot]),
            ]
        return copies

    def firsts(i):
        return [row_base + order_s[i * per + p] * rows for p in range(per)]

    def head_mask(h):
        return (lane >= h * size_h) & (lane < (h + 1) * size_h)

    masks = [head_mask(h) for h in range(heads)]

    def project(normed):
        proj = jnp.dot(normed, wp_ref[...], preferred_element_type=F32)
        query = (proj[:, :inner] * size_h ** (-0.5)).astype(BF16)
        keys = proj[:, inner : 2 * inner].astype(BF16)
        values = proj[:, 2 * inner : 3 * inner].astype(BF16)
        return query, keys, jnp.concatenate([values, jnp.ones_like(values)], 1), proj[:, 3 * inner :]

    def score_of(query, keys, mask, h):
        score = lax.dot_general(jnp.where(mask, query, zero), keys, NT, preferred_element_type=F32)
        return score * LOG2E + bias_s[h]

    def weigh(score, side):
        return jnp.dot(jnp.exp2(score).astype(BF16), side, preferred_element_type=F32)

    def gated_of(both, gate):
        return (jax.nn.sigmoid(gate) * (both[:, :inner] / both[:, inner:])).astype(BF16)

    def close(before, first, gated):
        update = jnp.dot(gated, wo_ref[...], preferred_element_type=F32)
        made = []
        for r, row in enumerate(first):
            at = slice(r * width, (r + 1) * width)
            place = lax.broadcasted_iota(jnp.int32, (width, chans), 0)
            live = (place < length) & (row < length)
            middle = before[at].astype(F32) + jnp.where(live, update[at], 0.0)
            made.append(middle.astype(BF16))
        return jnp.concatenate(made, 0)

    def finish(middle):
        middle = middle.astype(F32)
        normed_mid = normalise(middle).astype(BF16)
        hidden = jnp.dot(normed_mid, wu_ref[...], preferred_element_type=F32)
        hidden = jax.nn.relu(hidden).astype(BF16)
        down = jnp.dot(hidden, wd_ref[...], preferred_element_type=F32)
        return (middle + down).astype(BF16)

    def store(i, updated):
        out_ref[pl.ds(i * per, per)] = updated.reshape(per, rows, width, chans)

    def attend(i, slot, first):
        past = mid_s[...]
        query, keys, side, gate = project(n_s[slot].reshape(span, chans))
        ends = []
        for r in range(per * rows):
            at = slice(r * width, (r + 1) * width)
            both = None
            for h in range(heads):
                each = weigh(score_of(query[at], keys[at], masks[h], h), side[at])
                mask = jnp.concatenate([masks[h], masks[h]], 1)
                both = each if both is None else jnp.where(mask, each, both)
            ends.append(both)
        gated = gated_of(jnp.concatenate(ends, 0), gate)
        store(jnp.maximum(i - 1, 0), finish(past))
        mid_s[...] = close(
            x_s[slot].reshape(span, chans), [f + r for f in first for r in range(rows)], gated
        )
        low = functools.reduce(jnp.minimum, [e[:, inner:] for e in ends])
        high = functools.reduce(jnp.maximum, [e[:, inner:] for e in ends])
        low_s[...] = jnp.minimum(low_s[...], jnp.min(low.reshape(-1, 8, inner), 0))
        high_s[...] = jnp.maximum(high_s[...], jnp.max(high.reshape(-1, 8, inner), 0))

    for copy in fetches(0, 0):
        copy.start()
    for h in range(heads):
        bias_s[h] = jnp.where(keys_live, bias_ref[h].astype(F32) * LOG2E, DEAD)
    low_s[...] = jnp.ones_like(low_s)
    high_s[...] = jnp.ones_like(high_s)
    mid_s[...] = jnp.zeros_like(mid_s)
    def one_block(i, carry):
        slot = lax.rem(i, 2)
        first = firsts(i)
        some = functools.reduce(jnp.minimum, first) < length

        @pl.when(i + 1 < steps)
        def _():
            for copy in fetches(i + 1, 1 - slot):
                copy.start()

        for copy in fetches(i, slot):
            copy.wait()

        @pl.when(some)
        def _():
            attend(i, slot, first)

        @pl.when(jnp.logical_not(some))
        def _():
            store(jnp.maximum(i - 1, 0), finish(mid_s[...]))
            mid_s[...] = x_s[slot].reshape(span, chans)

        return carry

    lax.fori_loop(0, steps, one_block, 0)
    store(steps - 1, finish(mid_s[...]))
    good = (jnp.min(low_s[...]) > 1e-20) & (jnp.max(high_s[...]) < 1e30)

    @pl.when(jnp.logical_not(good))
    def _():
        def again(i, carry):
            for copy in fetches(i, 0):
                copy.start()
            for copy in fetches(i, 0):
                copy.wait()

            def one_row(r, carry):
                p = r // rows
                row = row_base + order_s[i * per + p] * rows + lax.rem(r, rows)
                query, keys, side, gate = project(n_s[0, p, lax.rem(r, rows)])

                def one_head(h, carry):
                    mask = head_mask(h)
                    score = score_of(query, keys, mask, h)
                    each = weigh(score - jnp.max(score, -1, keepdims=True), side)
                    sum_s[...] = jnp.where(jnp.concatenate([mask, mask], 1), each, sum_s[...])
                    return carry

                lax.fori_loop(0, heads, one_head, 0)
                gated = gated_of(sum_s[...], gate)
                middle = close(x_s[0, p, lax.rem(r, rows)], [row], gated)
                out_ref[i * per + p, lax.rem(r, rows)] = finish(middle)
                return carry

            lax.fori_loop(0, per * rows, one_row, 0)
            return carry

        lax.fori_loop(0, steps, again, 0)


def update_blocks(groups, lengths, info, blocks, normeds, bias, w_proj, w_out, w_up, w_down):
    count, rows, width, chans = blocks.shape
    inner = w_proj.shape[1] // 4
    per = 2
    vmem = pl.BlockSpec(memory_space=pltpu.VMEM)
    smem = pl.BlockSpec(memory_space=pltpu.SMEM)
    hbm = pl.BlockSpec(memory_space=pltpu.HBM)
    return pl.pallas_call(
        update_kernel,
        name="update",
        in_specs=[smem, smem, smem, hbm, hbm] + [vmem] * 5,
        out_specs=vmem,
        out_shape=jax.ShapeDtypeStruct((count, rows, width, chans), BF16),
        scratch_shapes=[
            pltpu.SMEM((count,), jnp.int32),
            pltpu.VMEM(bias.shape, F32),
            pltpu.VMEM((2, per, rows, width, chans), BF16),
            pltpu.VMEM((2, per, rows, width, chans), BF16),
            pltpu.VMEM((per * rows * width, chans), BF16),
            pltpu.VMEM((width, 2 * inner), F32),
            pltpu.VMEM((8, inner), F32),
            pltpu.VMEM((8, inner), F32),
            pltpu.SemaphoreType.DMA((2, per, 2)),
        ],
        compiler_params=pltpu.CompilerParams(vmem_limit_bytes=56 * 1024 * 1024),
    )(groups, lengths, info, blocks, normeds, bias, w_proj, w_out, w_up, w_down)


def shards(pair, lengths, block_group, w_proj, w_bias, w_out, w_up, w_down):
    group_idx = lax.axis_index("sample")
    axial_idx = lax.axis_index("axial")
    groups_n = lax.axis_size("sample")
    _, ax_rows, width, chans = pair.shape
    blk_rows = ax_rows // groups_n
    local = pair[0]
    info = jnp.stack([group_idx, axial_idx * ax_rows]).astype(jnp.int32)
    normed, bias = local_bias(local, w_bias)
    crop_bias = lax.all_gather(bias, "axial", axis=1, tiled=True)
    shape = (groups_n, blk_rows, width, chans)
    updated = update_blocks(
        block_group,
        lengths,
        info,
        local.reshape(shape),
        normed.reshape(shape),
        crop_bias,
        w_proj,
        w_out,
        w_up,
        w_down,
    )
    arrived = lax.all_to_all(updated, "sample", split_axis=0, concat_axis=0, tiled=True)
    return arrived.reshape(1, 1, groups_n, blk_rows, width, chans)


def solution(mesh):
    return jax.shard_map(
        shards,
        mesh=mesh,
        in_specs=(P("sample", "axial", None, None), P(), P(), P(), P(), P(), P(), P()),
        out_specs=P("sample", "axial", None, None, None, None),
        check_vma=False,
    )
```
